128 devices in a mesh: blk: 16 (over y, z_lo, core), grp: 8 (over x, z_hi).
Axes of the slice: x: 4, y: 4, z: 4 (z_hi: 2, z_lo: 2; z = z_hi * 2 + z_lo), core: 2. Of those that a mesh axis runs over, the one named last changes fastest.
Arguments:
- image_embed: float32 [24576, 1152], P(('blk', 'grp')), may hold values from -0.3125 to 0.3125
- text_embed: float32 [24576, 1152], P(('blk', 'grp')), may hold values from -0.3125 to 0.3125
- scale_parameter: float32 [1], replicated, may hold values from 3 to 10
- logit_bias: float32 [1], replicated, may hold values from -5 to -2
Outputs:
- image_gradient_scaled: float32 [24576, 1152], P(('blk', 'grp'))
- text_gradient_scaled: float32 [24576, 1152], P(('blk', 'grp'))
- window_mean_loss: float32 [1], replicated
The draws below stay inside these ranges and needn't reach their ends.
All inputs are finite; a program needn't handle non-finite values.
Results may differ from the reference program's by a relative error of at most 0.0004.
The reference program's roundings to bfloat16 on the way count: a program that leaves them out, or rounds other values in their place, can miss the bound.
Values may be sent and summed in bfloat16 or wider, within the bound.
No kernel may reach another device: no remote copies, remote signals or barrier semaphores. Data moves between devices by JAX's collectives and lax.ppermute only.
A program may use at most 128 MiB of HBM per device.

```python
import math
import jax
import jax.numpy as jnp
from jax import lax

EMBED_WIDTH = 1152
TOK_DEV = 192
STEPS = 3
PAIR_TOTAL = 24576
N_BLK = 16
N_GRP = 8


def block_scale(key, extent, pieces, least, largest):
    def one(axis_at, blocks):
        draws = jax.random.uniform(jax.random.fold_in(jax.random.fold_in(key, 6), axis_at), (blocks,), jnp.float32, least / len(pieces), largest / len(pieces))
        return jnp.repeat(jnp.exp(draws), extent[axis_at] // blocks).reshape((-1,) + (1,) * (len(extent) - axis_at - 1))

    factor_of = one(*pieces[0])
    for cut in pieces[1:]:
        factor_of = factor_of * one(*cut)
    return factor_of


def centred(rng, shape, deviation, bound, cuts=(), kind=jnp.bfloat16):
    gain = block_scale(rng, shape, cuts, -0.22, 0.18) if cuts else 1.0
    result = jax.random.normal(rng, shape, jnp.float32) * deviation * gain
    return jnp.minimum(jnp.maximum(result, -bound), bound).astype(kind)


def setup_inputs(seed: int = 0) -> dict:
    key_of = jax.random.split(jax.random.key(seed), 5)
    return {
        "image_embed": centred(key_of[0], (PAIR_TOTAL, EMBED_WIDTH), 0.05, 0.3125, ((0, 128),), jnp.float32),
        "text_embed": centred(key_of[1], (PAIR_TOTAL, EMBED_WIDTH), 0.05, 0.3125, ((0, 128),), jnp.float32),
        "scale_parameter": jnp.clip(jnp.exp(jax.random.uniform(key_of[2], (1,), jnp.float32, math.log(3.0), math.log(10.0))), 3.0, 10.0),
        "logit_bias": jnp.clip(jax.random.uniform(key_of[3], (1,), jnp.float32, -5.0, -2.0), -5.0, -2.0),
    }


def reference(image_embed, text_embed, scale_parameter, logit_bias):
    group_rows = N_GRP * TOK_DEV
    image_round = lax.optimization_barrier(image_embed.astype(jnp.bfloat16))
    text_round = lax.optimization_barrier(text_embed.astype(jnp.bfloat16))
    image_groups = image_round.astype(jnp.float32).reshape(N_BLK, group_rows, EMBED_WIDTH)
    text_groups = text_round.astype(jnp.float32).reshape(N_BLK, group_rows, EMBED_WIDTH)
    inverse_temp = scale_parameter[0]
    bias_offset = logit_bias[0]
    matches = jnp.eye(group_rows, dtype=jnp.float32)
    image_running_sum = jnp.zeros((N_BLK, group_rows, EMBED_WIDTH), jnp.float32)
    text_running_sum = jnp.zeros((N_BLK, group_rows, EMBED_WIDTH), jnp.float32)
    loss_total = jnp.zeros((), jnp.float32)
    for turn_index in range(STEPS):
        text_turned = jnp.roll(text_groups, turn_index, axis=0)
        similarity_matrix = jnp.einsum("gid,gjd->gij", image_groups, text_turned)
        pair_logits = inverse_temp * similarity_matrix + bias_offset
        if turn_index == 0:
            weights_full = jax.nn.sigmoid(pair_logits) - matches
            signed = pair_logits - 2.0 * matches * pair_logits
        else:
            weights_full = jax.nn.sigmoid(pair_logits)
            signed = pair_logits
        loss_total = loss_total + jnp.sum(jax.nn.softplus(signed))
        weights_round = lax.optimization_barrier(weights_full.astype(jnp.bfloat16))
        weights = weights_round.astype(jnp.float32)
        image_running_sum = image_running_sum + jnp.einsum("gij,gjd->gid", weights, text_turned)
        text_part = jnp.einsum("gij,gid->gjd", weights, image_groups)
        text_running_sum = text_running_sum + jnp.roll(text_part, -turn_index, axis=0)
    image_gradient_scaled = (inverse_temp * image_running_sum).reshape(PAIR_TOTAL, EMBED_WIDTH)
    text_gradient_scaled = (inverse_temp * text_running_sum).reshape(PAIR_TOTAL, EMBED_WIDTH)
    window_mean_loss = (loss_total / (PAIR_TOTAL * STEPS * group_rows)).reshape(1)
    return image_gradient_scaled, text_gradient_scaled, window_mean_loss
```

```python
import jax
import jax.numpy as jnp
from jax import lax
from jax.sharding import PartitionSpec as P

AXES = ("blk", "grp")
NY, NX = 4, 4
SEND_SCALE = 64.0


def place(y, z, core, x):
    z = z % 4
    return (((y % NY) * 2 + z % 2) * 2 + core % 2) * 8 + (x % NX) * 2 + z // 2


def route(move):
    pairs = []
    for y in range(NY):
        for z in range(4):
            for core in range(2):
                for x in range(NX):
                    pairs.append((place(y, z, core, x), place(*move(y, z, core, x))))
    return pairs


def along_x(k):
    return route(lambda y, z, core, x: (y, z, core, x + k))


def along_z(k):
    return route(lambda y, z, core, x: (y, z + k, core, x))


def along_y(k):
    return route(lambda y, z, core, x: (y + k, z, core, x))


def next_column(k, flip_zh, flip_core):
    def move(y, z, core, x):
        zh, zl = z // 2, z % 2
        column = (y * 2 + zl + k) % 8
        return column // 2, (zh ^ flip_zh) * 2 + column % 2, core ^ flip_core, x

    return route(move)


OTHER_CORE = route(lambda y, z, core, x: (y, z, core + 1, x))


def send(value, pairs):
    return lax.ppermute(value, AXES, pairs)


def total_over_devices(value):
    value = value + send(value, OTHER_CORE)
    for axis in (along_x, along_z, along_y):
        value = value + send(value, axis(1)) + send(value, axis(2)) + send(value, axis(3))
    return value


def local(image_embed, text_embed, scale_parameter, logit_bias):
    n = image_embed.shape[0]
    scale = scale_parameter[0]
    bias = logit_bias[0]
    core = lax.axis_index("blk") % 2
    image_b = image_embed.astype(jnp.bfloat16)
    text_b = text_embed.astype(jnp.bfloat16)

    text_z = send(text_b, along_z(2))
    far_a = send(text_b, next_column(1, 0, 1))
    far_b = send(text_b, next_column(1, 1, 1))
    image_l = send(image_b, along_x(1))
    image_r = send(image_b, along_x(-1))
    image_f = send(image_b, along_x(2))
    images = jnp.concatenate([image_b, image_l, image_r, image_f])
    text_0 = jnp.concatenate([text_b, text_z])
    far = jnp.concatenate([far_a, far_b])
    text_2 = send(far, OTHER_CORE)
    text_1 = jnp.where(core == 0, far, send(text_0, OTHER_CORE))

    contract_last = (((1,), (1,)), ((), ()))
    contract_first = (((0,), (0,)), ((), ()))
    loss = jnp.zeros((), jnp.float32)
    weights = []
    sums = []
    for s, text in enumerate((text_0, text_1, text_2)):
        logits = scale * lax.dot_general(
            images, text, contract_last, preferred_element_type=jnp.float32
        ) + bias
        probs = jax.nn.sigmoid(logits)
        signed = logits
        if s == 0:
            row = lax.broadcasted_iota(jnp.int32, logits.shape, 0)
            col = lax.broadcasted_iota(jnp.int32, logits.shape, 1)
            match = ((row == col) & (row < n)).astype(jnp.float32)
            probs = probs - match
            signed = logits - 2.0 * match * logits
        loss = loss + jnp.sum(jax.nn.softplus(signed))
        w = probs.astype(jnp.bfloat16)
        weights.append(w)
        sums.append(
            lax.dot_general(w, images, contract_first, preferred_element_type=jnp.float32)
        )
    loss_total = total_over_devices(jnp.broadcast_to(loss, (8, 128)))

    def narrow(value):
        return (value * SEND_SCALE).astype(jnp.float16)

    def wide(value):
        return value.astype(jnp.float32) * (1.0 / SEND_SCALE)

    sum_0, sum_1, sum_2 = sums
    swapped = send(sum_1, OTHER_CORE)
    sum_0 = sum_0 + jnp.where(core == 0, swapped, 0.0)
    sum_2 = sum_2 + jnp.where(core == 1, swapped, 0.0)
    back_z = send(narrow(sum_0[n:]), along_z(2))
    back_a = send(narrow(sum_2[:n]), next_column(-1, 0, 0))
    back_b = send(narrow(sum_2[n:]), next_column(-1, 1, 0))
    text_sum = sum_0[:n] + wide(back_z) + wide(back_a) + wide(back_b)

    image_sum = jnp.dot(
        jnp.concatenate(weights, axis=1),
        jnp.concatenate([text_0, text_1, text_2]),
        preferred_element_type=jnp.float32,
    )
    home_l = send(narrow(image_sum[n : 2 * n]), along_x(-1))
    home_r = send(narrow(image_sum[2 * n : 3 * n]), along_x(1))
    home_f = send(narrow(image_sum[3 * n :]), along_x(2))
    image_own = image_sum[:n] + wide(home_l) + wide(home_r) + wide(home_f)

    pair_count = 128 * n * 3 * 8 * n
    mean_loss = (loss_total[0, 0] / pair_count).reshape(1)
    return scale * image_own, scale * text_sum, mean_loss


def solution(mesh):
    placed = (P(("blk", "grp"), None), P(("blk", "grp"), None), P(), P())
    return jax.shard_map(
        local,
        mesh=mesh,
        in_specs=placed,
        out_specs=(P(("blk", "grp"), None), P(("blk", "grp"), None), P()),
        check_vma=False,
    )
```

```python
import functools

import jax
import jax.numpy as jnp
from jax import lax
from jax.experimental import pallas as pl
from jax.experimental.pallas import tpu as pltpu
from jax.sharding import Mesh
from jax.sharding import PartitionSpec as P

AXES = ("y", "z_lo", "core", "x", "z_hi")
CHIPS = ("y", "z_lo", "x", "z_hi")
NY, NX = 4, 4
DEVICES = 128
CHIP_COUNT = 64
SEND_SCALE = 64.0
LAST = (((1,), (1,)), ((), ()))
FIRST = (((0,), (0,)), ((), ()))
PLAIN = (((1,), (0,)), ((), ()))
VMEM_BYTES = 16 * 1024 * 1024


def place(y, z, core, x):
    z = z % 4
    return (((y % NY) * 2 + z % 2) * 2 + core % 2) * 8 + (x % NX) * 2 + z // 2


def route(move):
    pairs = []
    for y in range(NY):
        for z in range(4):
            for core in range(2):
                for x in range(NX):
                    pairs.append((place(y, z, core, x), place(*move(y, z, core, x))))
    return pairs


def along_x(k):
    return route(lambda y, z, core, x: (y, z, core, x + k))


def along_z(k):
    return route(lambda y, z, core, x: (y, z + k, core, x))


def next_column(k, flip_zh):
    def move(y, z, core, x):
        zh, zl = z // 2, z % 2
        column = (y * 2 + zl + k) % 8
        return column // 2, (zh ^ flip_zh(core)) * 2 + column % 2, core, x

    return route(move)


ACROSS = route(lambda y, z, core, x: (y, z, core, x + 1 - 2 * core))
OTHER_CORE = route(lambda y, z, core, x: (y, z, core + 1, x))


def send(value, pairs):
    return lax.ppermute(value, AXES, pairs)


def dot(a, b, dims):
    return lax.dot_general(a, b, dims, preferred_element_type=jnp.float32)


WHOLE = pl.BlockSpec(memory_space=pltpu.VMEM)
SCALAR = pl.BlockSpec(memory_space=pltpu.SMEM)


def call(body, outs, ins, flops, transcendentals=0, scalars=1):
    return pl.pallas_call(
        body,
        out_shape=tuple(jax.ShapeDtypeStruct(s, t) for s, t in outs),
        in_specs=[SCALAR] * scalars + [WHOLE] * (len(ins) - scalars),
        out_specs=(WHOLE,) * len(outs),
        compiler_params=pltpu.CompilerParams(vmem_limit_bytes=VMEM_BYTES),
        cost_estimate=pl.CostEstimate(
            flops=flops, bytes_accessed=1 << 20, transcendentals=transcendentals
        ),
    )(*ins)


def pair_weights(scalars, images, text, weights, part, total, labelled):
    z = scalars[0] * dot(text, images[...], LAST) + scalars[1]
    e = jnp.exp(-jnp.abs(z))
    r = 1.0 / (1.0 + e)
    p = jnp.where(z >= 0.0, r, e * r)
    top = jnp.maximum(z, 0.0)
    if labelled:
        row = lax.broadcasted_iota(jnp.int32, z.shape, 0)
        col = lax.broadcasted_iota(jnp.int32, z.shape, 1)
        match = (row == col).astype(jnp.float32)
        p = p - match
        top = top - match * z
    rows, cols = z.shape
    total = total + jnp.sum(top.reshape(rows // 8, 8, cols), axis=0)
    e = e.reshape(rows // 8, 8, cols)
    for first in range(0, rows // 8, 8):
        q = e[first]
        for k in range(first + 1, min(first + 8, rows // 8)):
            q = q + (e[k] + q * e[k])
        total = total + jnp.log1p(q)
    weights[part, :] = p.astype(jnp.bfloat16)
    return total


def fold(total):
    out = total[:, :128]
    for k in range(128, total.shape[1], 128):
        out = out + total[:, k : k + 128]
    return out


def near_body(scalars, i0, i1, i2, i3, ta, tb, images, weights, loss):
    n = ta.shape[0]
    for k, ref in enumerate((i0, i1, i2, i3)):
        images[pl.ds(k * n, n), :] = ref[...]
    total = jnp.zeros((8, 4 * n), jnp.float32)
    total = pair_weights(scalars, images, ta[...], weights, pl.ds(0, n), total, True)
    total = pair_weights(scalars, images, tb[...], weights, pl.ds(n, n), total, False)
    loss[...] = fold(total)


def far_body(scalars, core, images, ta, tb, w0, own_o, z_o, far, far_o, loss_0, t1, t2, w1, w2, across, sum_1, loss):
    n = own_o.shape[0]
    low, high, last = pl.ds(0, n), pl.ds(n, n), pl.ds(3 * n, n)
    first = core[0] == 0
    total = jnp.zeros((8, 4 * n), jnp.float32)
    t1[low, :] = jnp.where(first, far[high, :], own_o[...])
    total = pair_weights(scalars, images, t1[low, :], w1, low, total, False)
    t1[high, :] = jnp.where(first, far_o[high, :], z_o[...])
    total = pair_weights(scalars, images, t1[high, :], w1, high, total, False)
    sum_1[low, :] = dot(w1[low, :], images[...], PLAIN)
    t2[low, :] = jnp.where(first, far[low, :], far_o[high, :])
    total = pair_weights(scalars, images, t2[low, :], w2, low, total, False)
    sum_1[high, :] = dot(w1[high, :], images[...], PLAIN)
    t2[high, :] = jnp.where(first, far_o[low, :], far[high, :])
    total = pair_weights(scalars, images, t2[high, :], w2, high, total, False)
    across[...] = image_sum(last, w0, w1, w2, ta, tb, t1, t2)
    loss[...] = loss_0[...] + fold(total)


def image_sum(cut, w0, w1, w2, ta, tb, t1, t2):
    n = ta.shape[0]
    total = dot(w0[pl.ds(0, n), cut], ta[...], FIRST)
    total = total + dot(w0[pl.ds(n, n), cut], tb[...], FIRST)
    total = total + dot(w1[:, cut], t1[...], FIRST)
    return total + dot(w2[:, cut], t2[...], FIRST)


def rest_body(images, w0, w1, w2, ta, tb, t1, t2, sum_a, sum_b, sum_2, own, left, right):
    n = ta.shape[0]
    sum_a[...] = dot(w0[pl.ds(0, n), :], images[...], PLAIN)
    sum_b[...] = dot(w0[pl.ds(n, n), :], images[...], PLAIN)
    for k in range(2):
        part = pl.ds(k * n, n)
        sum_2[part, :] = dot(w2[part, :], images[...], PLAIN)
    for k, out in enumerate((own, left, right)):
        out[...] = image_sum(pl.ds(k * n, n), w0, w1, w2, ta, tb, t1, t2)


def narrow(value):
    return (value * SEND_SCALE).astype(jnp.float16)


def wide(value):
    return value.astype(jnp.float32) * (1.0 / SEND_SCALE)


def local(image_embed, text_embed, scale_parameter, logit_bias):
    n, width = image_embed.shape
    scale = scale_parameter[0]
    scalars = jnp.concatenate([scale_parameter, logit_bias])
    core = lax.axis_index("core").astype(jnp.int32).reshape(1)
    first_core = core[0] == 0
    bf16, f32 = jnp.bfloat16, jnp.float32
    unit = 2 * n * 4 * n * width

    text_b = text_embed.astype(bf16)
    image_b = image_embed.astype(bf16)
    text_o = send(text_b, OTHER_CORE)
    both = jnp.where(
        first_core,
        jnp.concatenate([text_b, text_o]),
        jnp.concatenate([text_o, text_b]),
    )
    far = send(both, next_column(1, lambda core: core))
    text_z = send(text_b, along_z(2))
    image_l = send(image_b, along_x(1))
    image_r = send(image_b, along_x(-1))
    image_f = send(image_b, along_x(2))
    far, text_z, image_l, image_r, image_f, scalars, core = lax.optimization_barrier(
        (far, text_z, image_l, image_r, image_f, scalars, core)
    )
    z_o = send(text_z, OTHER_CORE)
    far_o = send(far, OTHER_CORE)

    images, w0, loss_0 = call(
        near_body,
        [((4 * n, width), bf16), ((2 * n, 4 * n), bf16), ((8, 128), f32)],
        (scalars, image_b, image_l, image_r, image_f, text_b, text_z),
        4 * unit,
    )
    t1, t2, w1, w2, across, sum_1, loss = call(
        far_body,
        [((2 * n, width), bf16)] * 2
        + [((2 * n, 4 * n), bf16)] * 2
        + [((n, width), f32), ((2 * n, width), f32), ((8, 128), f32)],
        (scalars, core, images, text_b, text_z, w0, text_o, z_o, far, far_o, loss_0),
        8 * unit,
        scalars=2,
    )
    passed = send(narrow(across), ACROSS)
    swapped = send(narrow(sum_1), OTHER_CORE)
    sum_a, sum_b, sum_2, own, left, right = call(
        rest_body,
        [((n, width), f32)] * 2 + [((2 * n, width), f32)] + [((n, width), f32)] * 3,
        (images, w0, w1, w2, text_b, text_z, t1, t2),
        7 * unit,
        scalars=0,
    )
    passed = wide(passed)
    swapped = wide(swapped)
    to_first = jnp.where(first_core, swapped, 0.0)
    sum_a = sum_a + to_first[:n]
    sum_b = sum_b + to_first[n:]
    sum_2 = sum_2 + jnp.where(first_core, 0.0, swapped)
    left = left + jnp.where(first_core, 0.0, passed)
    right = right + jnp.where(first_core, passed, 0.0)
    loss = loss + send(loss, OTHER_CORE)
    out = lax.optimization_barrier(
        tuple(narrow(v) for v in (sum_b, sum_2[:n], sum_2[n:]))
    )
    out = out + lax.optimization_barrier((narrow(left), narrow(right), loss))
    back_z = send(out[0], along_z(2))
    back_a = send(out[1], next_column(-1, lambda core: 0))
    back_b = send(out[2], next_column(-1, lambda core: 1))
    home_l = send(out[3], along_x(-1))
    home_r = send(out[4], along_x(1))

    loss = jnp.broadcast_to(jnp.sum(out[5]), (CHIP_COUNT, 1, 128))
    losses = lax.all_to_all(loss, CHIPS, 0, 0, tiled=True)
    pair_count = DEVICES * n * 3 * 8 * n
    mean_loss = (jnp.sum(losses[:, 0, 0]) / pair_count).reshape(1)
    text_out = scale * (sum_a + wide(back_z) + wide(back_a) + wide(back_b))
    own, text_out = lax.optimization_barrier((own, text_out))
    image_out = scale * (own + wide(home_l) + wide(home_r))
    return image_out, text_out, mean_loss


def solution(mesh):
    fine = Mesh(mesh.devices.reshape(NY, 2, 2, NX, 2), AXES)
    placed = (P(AXES, None), P(AXES, None), P(), P())
    return jax.shard_map(
        local,
        mesh=fine,
        in_specs=placed,
        out_specs=(P(AXES, None), P(AXES, None), P()),
        check_vma=False,
    )
```

```python
import functools

import jax
import jax.numpy as jnp
from jax import lax
from jax.experimental import pallas as pl
from jax.experimental.pallas import tpu as pltpu
from jax.sharding import Mesh
from jax.sharding import PartitionSpec as P

AXES = ("y", "z_lo", "core", "x", "z_hi")
CHIPS = ("y", "z_lo", "x", "z_hi")
NY, NX = 4, 4
DEVICES = 128
CHIP_COUNT = 64
SEND_SCALE = 64.0
TILE = 64
LAST = (((1,), (1,)), ((), ()))
FIRST = (((0,), (0,)), ((), ()))
PLAIN = (((1,), (0,)), ((), ()))
VMEM_BYTES = 16 * 1024 * 1024


def place(y, z, core, x):
    z = z % 4
    return (((y % NY) * 2 + z % 2) * 2 + core % 2) * 8 + (x % NX) * 2 + z // 2


def route(move):
    pairs = []
    for y in range(NY):
        for z in range(4):
            for core in range(2):
                for x in range(NX):
                    pairs.append((place(y, z, core, x), place(*move(y, z, core, x))))
    return pairs


def along_x(k):
    return route(lambda y, z, core, x: (y, z, core, x + k))


def along_z(k):
    return route(lambda y, z, core, x: (y, z + k, core, x))


def next_column(k, flip_zh):
    def move(y, z, core, x):
        zh, zl = z // 2, z % 2
        column = (y * 2 + zl + k) % 8
        return column // 2, (zh ^ flip_zh(core)) * 2 + column % 2, core, x

    return route(move)


ACROSS = route(lambda y, z, core, x: (y, z, core, x + 1 - 2 * core))
OTHER_CORE = route(lambda y, z, core, x: (y, z, core + 1, x))


def send(value, pairs):
    return lax.ppermute(value, AXES, pairs)


def dot(a, b, dims):
    return lax.dot_general(a, b, dims, preferred_element_type=jnp.float32)


WHOLE = pl.BlockSpec(memory_space=pltpu.VMEM)
SCALAR = pl.BlockSpec(memory_space=pltpu.SMEM)


def call(body, outs, ins, flops, scalars=1, scratch=()):
    return pl.pallas_call(
        body,
        out_shape=tuple(jax.ShapeDtypeStruct(s, t) for s, t in outs),
        in_specs=[SCALAR] * scalars + [WHOLE] * (len(ins) - scalars),
        out_specs=(WHOLE,) * len(outs),
        scratch_shapes=scratch,
        compiler_params=pltpu.CompilerParams(vmem_limit_bytes=VMEM_BYTES),
        cost_estimate=pl.CostEstimate(
            flops=flops, bytes_accessed=1 << 20, transcendentals=0
        ),
    )(*ins)


def tile_terms(scalars, z, match):
    z = scalars[0] * z + scalars[1]
    e = jnp.exp(-jnp.abs(z))
    d = 1.0 + e
    r = pltpu.reciprocal(d, approx=True)
    r = r * (2.0 - d * r)
    p = r * jnp.where(z >= 0.0, 1.0, e)
    top = jnp.maximum(z, 0.0)
    if match is not None:
        p = p - match
        top = top - match * z
    rows, cols = z.shape
    total = jnp.sum(top.reshape(rows // 8, 8, cols), axis=0)
    e = e.reshape(rows // 8, 8, cols)
    d = d.reshape(rows // 8, 8, cols)
    q = e[0]
    for k in range(1, rows // 8):
        q = q * d[k] + e[k]
    return p.astype(jnp.bfloat16), total + jnp.log1p(q)


def pair_weights(scalars, images, text, weights, products, loss, labelled):
    step = products.shape[2]
    rows, cols = weights.shape
    own = rows // 2

    def multiply(k):
        products[k % 2, :, :] = dot(text, images[pl.ds(k * step, step), :], LAST)

    multiply(0)
    for k in range(cols // step):
        if (k + 1) * step < cols:
            multiply(k + 1)
        for r in range(0, rows, TILE):
            for c in range(0, step, 128):
                match = None
                at = k * step + c
                if labelled and r < own and at < own and at < r + TILE and r < at + 128:
                    row = lax.broadcasted_iota(jnp.int32, (TILE, 128), 0) + r
                    col = lax.broadcasted_iota(jnp.int32, (TILE, 128), 1) + at
                    match = ((row == col) & (row < own)).astype(jnp.float32)
                part, terms = tile_terms(
                    scalars, products[k % 2, pl.ds(r, TILE), pl.ds(c, 128)], match
                )
                weights[pl.ds(r, TILE), pl.ds(at, 128)] = part
                loss = loss + terms
    return loss


def near_body(scalars, i0, i1, i2, i3, ta, tb, images, text, weights, loss, products):
    n = ta.shape[0]
    for k, ref in enumerate((i0, i1, i2, i3)):
        images[pl.ds(k * n, n), :] = ref[...]
    text[pl.ds(0, n), :] = ta[...]
    text[pl.ds(n, n), :] = tb[...]
    none = jnp.zeros((8, 128), jnp.float32)
    loss[...] = pair_weights(scalars, images, text[...], weights, products, none, True)


def far_body(scalars, core, images, t0, w0, own_o, z_o, far, far_o, loss_0, text, weights, across, sum_1, loss, products):
    n = own_o.shape[0]
    low, high, last = pl.ds(0, n), pl.ds(n, n), pl.ds(3 * n, n)
    first = core[0] == 0
    text[pl.ds(0, n), :] = jnp.where(first, far[high, :], own_o[...])
    text[pl.ds(n, n), :] = jnp.where(first, far_o[high, :], z_o[...])
    text[pl.ds(2 * n, n), :] = jnp.where(first, far[low, :], far_o[high, :])
    text[pl.ds(3 * n, n), :] = jnp.where(first, far_o[low, :], far[high, :])
    loss[...] = pair_weights(scalars, images, text[...], weights, products, loss_0[...], False)
    sum_1[...] = dot(weights[pl.ds(0, 2 * n), :], images[...], PLAIN)
    across[...] = dot(w0[:, last], t0[...], FIRST) + dot(weights[:, last], text[...], FIRST)


def text_body(images, w0, weights, sum_a, sum_b, sum_2):
    n = sum_a.shape[0]
    out = dot(w0[...], images[...], PLAIN)
    sum_a[...] = out[:n]
    sum_b[...] = out[n:]
    sum_2[...] = dot(weights[pl.ds(2 * n, 2 * n), :], images[...], PLAIN)


def image_body(w0, weights, t0, text, *outs):
    n = outs[0].shape[0]
    cut = pl.ds(0, len(outs) * n)
    out = dot(w0[:, cut], t0[...], FIRST) + dot(weights[:, cut], text[...], FIRST)
    for k, ref in enumerate(outs):
        ref[...] = out[k * n : (k + 1) * n]


def spread_body(mine, other, out):
    total = jnp.sum(mine[...] + other[...])
    out[...] = jnp.full(out.shape, total, jnp.float32)


def total_body(parts, out):
    out[...] = jnp.broadcast_to(jnp.sum(parts[...], axis=0), out.shape)


def narrow(value):
    return (value * SEND_SCALE).astype(jnp.float16)


def wide(value):
    return value.astype(jnp.float32) * (1.0 / SEND_SCALE)


def local(image_embed, text_embed, scale_parameter, logit_bias):
    n, width = image_embed.shape
    scale = scale_parameter[0]
    scalars = jnp.concatenate([scale_parameter, logit_bias])
    core = lax.axis_index("core").astype(jnp.int32).reshape(1)
    first_core = core[0] == 0
    bf16, f32 = jnp.bfloat16, jnp.float32
    unit = 2 * n * 4 * n * width

    text_b = text_embed.astype(bf16)
    image_b = image_embed.astype(bf16)
    text_o = send(text_b, OTHER_CORE)
    both = jnp.where(
        first_core,
        jnp.concatenate([text_b, text_o]),
        jnp.concatenate([text_o, text_b]),
    )
    far = send(both, next_column(1, lambda core: core))
    text_z = send(text_b, along_z(2))
    image_l = send(image_b, along_x(1))
    image_r = send(image_b, along_x(-1))
    image_f = send(image_b, along_x(2))
    far, text_z, image_l, image_r, image_f, scalars, core = lax.optimization_barrier(
        (far, text_z, image_l, image_r, image_f, scalars, core)
    )
    z_o = send(text_z, OTHER_CORE)
    far_o = send(far, OTHER_CORE)

    images, t0, w0, loss_0 = call(
        near_body,
        [((4 * n, width), bf16), ((2 * n, width), bf16), ((2 * n, 4 * n), bf16), ((8, 128), f32)],
        (scalars, image_b, image_l, image_r, image_f, text_b, text_z),
        2 * unit,
        scratch=[pltpu.VMEM((2, 2 * n, 2 * n), f32)],
    )
    text, weights, across, sum_1, loss = call(
        far_body,
        [
            ((4 * n, width), bf16),
            ((4 * n, 4 * n), bf16),
            ((n, width), f32),
            ((2 * n, width), f32),
            ((8, 128), f32),
        ],
        (scalars, core, images, t0, w0, text_o, z_o, far, far_o, loss_0),
        8 * unit,
        scalars=2,
        scratch=[pltpu.VMEM((2, 4 * n, 2 * n), f32)],
    )
    passed = send(narrow(across), ACROSS)
    swapped = send(narrow(sum_1), OTHER_CORE)
    sum_a, sum_b, sum_2 = call(
        text_body,
        [((n, width), f32)] * 2 + [((2 * n, width), f32)],
        (images, w0, weights),
        4 * unit,
        scalars=0,
    )
    passed = wide(passed)
    swapped = wide(swapped)
    to_first = jnp.where(first_core, swapped, 0.0)
    sum_b = sum_b + to_first[n:]
    sum_2 = sum_2 + jnp.where(first_core, 0.0, swapped)
    (loss,) = call(spread_body, [((CHIP_COUNT, 1, 128), f32)], (loss, send(loss, OTHER_CORE)), 4, scalars=0)
    out = lax.optimization_barrier(
        tuple(narrow(v) for v in (sum_b, sum_2[:n], sum_2[n:])) + (sum_a + to_first[:n], w0)
    )
    sum_a, w0 = out[3:]
    out = out[:3]
    own, left, right = call(
        image_body, [((n, width), f32)] * 3, (w0, weights, t0, text), 9 * unit // 2, scalars=0
    )
    left = left + jnp.where(first_core, 0.0, passed)
    right = right + jnp.where(first_core, passed, 0.0)
    out = out + lax.optimization_barrier((narrow(left), narrow(right), loss))
    back_z = send(out[0], along_z(2))
    back_a = send(out[1], next_column(-1, lambda core: 0))
    back_b = send(out[2], next_column(-1, lambda core: 1))
    home_l = send(out[3], along_x(-1))
    home_r = send(out[4], along_x(1))

    losses = lax.all_to_all(out[5], CHIPS, 0, 0, tiled=True)
    text_out = scale * (sum_a + wide(back_z) + wide(back_a) + wide(back_b))
    own, text_out = lax.optimization_barrier((own, text_out))
    image_out = scale * (own + wide(home_l) + wide(home_r))
    losses, image_out = lax.optimization_barrier((losses, image_out))
    pair_count = DEVICES * n * 3 * 8 * n
    mean_loss = call(total_body, [((8, 128), f32)], (losses,), 4, scalars=0)[0][0, :1] / pair_count
    return image_out, text_out, mean_loss


def solution(mesh):
    fine = Mesh(mesh.devices.reshape(NY, 2, 2, NX, 2), AXES)
    placed = (P(AXES, None), P(AXES, None), P(), P())
    return jax.shard_map(
        local,
        mesh=fine,
        in_specs=placed,
        out_specs=(P(AXES, None), P(AXES, None), P()),
        check_vma=False,
    )
```

```python
import functools

import jax
import jax.numpy as jnp
from jax import lax
from jax.experimental import pallas as pl
from jax.experimental.pallas import tpu as pltpu
from jax.sharding import Mesh
from jax.sharding import PartitionSpec as P

AXES = ("y", "z_lo", "core", "x", "z_hi")
CHIPS = ("y", "z_lo", "x", "z_hi")
NY, NX = 4, 4
DEVICES = 128
CHIP_COUNT = 64
SEND_SCALE = 64.0
TILE = 64
LAST = (((1,), (1,)), ((), ()))
FIRST = (((0,), (0,)), ((), ()))
PLAIN = (((1,), (0,)), ((), ()))
VMEM_BYTES = 16 * 1024 * 1024


def place(y, z, core, x):
    z = z % 4
    return (((y % NY) * 2 + z % 2) * 2 + core % 2) * 8 + (x % NX) * 2 + z // 2


def route(move):
    pairs = []
    for y in range(NY):
        for z in range(4):
            for core in range(2):
                for x in range(NX):
                    pairs.append((place(y, z, core, x), place(*move(y, z, core, x))))
    return pairs


def along_x(k):
    return route(lambda y, z, core, x: (y, z, core, x + k))


def along_z(k):
    return route(lambda y, z, core, x: (y, z + k, core, x))


def next_column(k, flip_zh):
    def move(y, z, core, x):
        zh, zl = z // 2, z % 2
        column = (y * 2 + zl + k) % 8
        return column // 2, (zh ^ flip_zh(core)) * 2 + column % 2, core, x

    return route(move)


ACROSS = route(lambda y, z, core, x: (y, z, core, x + 1 - 2 * core))
OTHER_CORE = route(lambda y, z, core, x: (y, z, core + 1, x))


def send(value, pairs):
    return lax.ppermute(value, AXES, pairs)


def dot(a, b, dims):
    return lax.dot_general(a, b, dims, preferred_element_type=jnp.float32)


WHOLE = pl.BlockSpec(memory_space=pltpu.VMEM)
SCALAR = pl.BlockSpec(memory_space=pltpu.SMEM)


def call(body, outs, ins, flops, scalars=1, scratch=()):
    return pl.pallas_call(
        body,
        out_shape=tuple(jax.ShapeDtypeStruct(s, t) for s, t in outs),
        in_specs=[SCALAR] * scalars + [WHOLE] * (len(ins) - scalars),
        out_specs=(WHOLE,) * len(outs),
        scratch_shapes=scratch,
        compiler_params=pltpu.CompilerParams(vmem_limit_bytes=VMEM_BYTES),
        cost_estimate=pl.CostEstimate(
            flops=flops, bytes_accessed=1 << 20, transcendentals=0
        ),
    )(*ins)


def tile_terms(scalars, z, match):
    z = scalars[0] * z + scalars[1]
    e = jnp.exp(-jnp.abs(z))
    d = 1.0 + e
    r = pltpu.reciprocal(d, approx=True)
    r = r * (2.0 - d * r)
    p = r * jnp.where(z >= 0.0, 1.0, e)
    top = jnp.maximum(z, 0.0)
    if match is not None:
        p = p - match
        top = top - match * z
    rows, cols = z.shape
    total = jnp.sum(top.reshape(rows // 8, 8, cols), axis=0)
    e = e.reshape(rows // 8, 8, cols)
    d = d.reshape(rows // 8, 8, cols)
    q = e[0]
    for k in range(1, rows // 8):
        q = q * d[k] + e[k]
    return p.astype(jnp.bfloat16), total + jnp.log1p(q)


def pair_weights(scalars, images, text, weights, products, loss, labelled):
    step = products.shape[2]
    rows, cols = weights.shape
    own = rows // 2

    def multiply(k):
        products[k % 2, :, :] = dot(text, images[pl.ds(k * step, step), :], LAST)

    multiply(0)
    for k in range(cols // step):
        if (k + 1) * step < cols:
            multiply(k + 1)
        for r in range(0, rows, TILE):
            for c in range(0, step, 128):
                match = None
                at = k * step + c
                if labelled and r < own and at < own and at < r + TILE and r < at + 128:
                    row = lax.broadcasted_iota(jnp.int32, (TILE, 128), 0) + r
                    col = lax.broadcasted_iota(jnp.int32, (TILE, 128), 1) + at
                    match = ((row == col) & (row < own)).astype(jnp.float32)
                part, terms = tile_terms(
                    scalars, products[k % 2, pl.ds(r, TILE), pl.ds(c, 128)], match
                )
                weights[pl.ds(r, TILE), pl.ds(at, 128)] = part
                loss = loss + terms
    return loss


def near_body(scalars, i0, i1, i2, i3, ta, tb, images, text, weights, loss, products):
    n = ta.shape[0]
    for k, ref in enumerate((i0, i1, i2, i3)):
        images[pl.ds(k * n, n), :] = ref[...]
    text[pl.ds(0, n), :] = ta[...]
    text[pl.ds(n, n), :] = tb[...]
    none = jnp.zeros((8, 128), jnp.float32)
    loss[...] = pair_weights(scalars, images, text[...], weights, products, none, True)


def far_body(scalars, core, images, t0, w0, own_o, z_o, far, far_o, loss_0, text, weights, across, sum_1, loss, products):
    n = own_o.shape[0]
    low, high, last = pl.ds(0, n), pl.ds(n, n), pl.ds(3 * n, n)
    first = core[0] == 0
    text[pl.ds(0, n), :] = jnp.where(first, far[high, :], own_o[...])
    text[pl.ds(n, n), :] = jnp.where(first, far_o[high, :], z_o[...])
    text[pl.ds(2 * n, n), :] = jnp.where(first, far[low, :], far_o[high, :])
    text[pl.ds(3 * n, n), :] = jnp.where(first, far_o[low, :], far[high, :])
    loss[...] = pair_weights(scalars, images, text[...], weights, products, loss_0[...], False)
    sum_1[...] = dot(weights[pl.ds(0, 2 * n), :], images[...], PLAIN)
    across[...] = dot(w0[:, last], t0[...], FIRST) + dot(weights[:, last], text[...], FIRST)


def text_body(images, w0, weights, sum_a, sum_b, sum_2):
    n = sum_a.shape[0]
    out = dot(w0[...], images[...], PLAIN)
    sum_a[...] = out[:n]
    sum_b[...] = out[n:]
    sum_2[...] = dot(weights[pl.ds(2 * n, 2 * n), :], images[...], PLAIN)


def image_body(w0, weights, t0, text, *outs):
    n = outs[0].shape[0]
    cut = pl.ds(0, len(outs) * n)
    out = dot(w0[:, cut], t0[...], FIRST) + dot(weights[:, cut], text[...], FIRST)
    for k, ref in enumerate(outs):
        ref[...] = out[k * n : (k + 1) * n]


def spread_body(mine, other, out):
    total = jnp.sum(mine[...] + other[...])
    out[...] = jnp.full(out.shape, total, jnp.float32)


def mean_body(pairs, parts, out):
    out[0] = jnp.sum(parts[...][:, 0, :1]) / pairs


def narrow(value):
    return (value * SEND_SCALE).astype(jnp.float16)


def wide(value):
    return value.astype(jnp.float32) * (1.0 / SEND_SCALE)


def local(image_embed, text_embed, scale_parameter, logit_bias):
    n, width = image_embed.shape
    scale = scale_parameter[0]
    scalars = jnp.concatenate([scale_parameter, logit_bias])
    core = lax.axis_index("core").astype(jnp.int32).reshape(1)
    first_core = core[0] == 0
    bf16, f32 = jnp.bfloat16, jnp.float32
    unit = 2 * n * 4 * n * width

    text_b = text_embed.astype(bf16)
    image_b = image_embed.astype(bf16)
    text_o = send(text_b, OTHER_CORE)
    both = jnp.where(
        first_core,
        jnp.concatenate([text_b, text_o]),
        jnp.concatenate([text_o, text_b]),
    )
    far = send(both, next_column(1, lambda core: core))
    text_z = send(text_b, along_z(2))
    image_l = send(image_b, along_x(1))
    image_r = send(image_b, along_x(-1))
    image_f = send(image_b, along_x(2))
    far, text_z, image_l, image_r, image_f, scalars, core = lax.optimization_barrier(
        (far, text_z, image_l, image_r, image_f, scalars, core)
    )
    z_o = send(text_z, OTHER_CORE)
    far_o = send(far, OTHER_CORE)

    images, t0, w0, loss_0 = call(
        near_body,
        [((4 * n, width), bf16), ((2 * n, width), bf16), ((2 * n, 4 * n), bf16), ((8, 128), f32)],
        (scalars, image_b, image_l, image_r, image_f, text_b, text_z),
        2 * unit,
        scratch=[pltpu.VMEM((2, 2 * n, 2 * n), f32)],
    )
    text, weights, across, sum_1, loss = call(
        far_body,
        [
            ((4 * n, width), bf16),
            ((4 * n, 4 * n), bf16),
            ((n, width), f32),
            ((2 * n, width), f32),
            ((8, 128), f32),
        ],
        (scalars, core, images, t0, w0, text_o, z_o, far, far_o, loss_0),
        8 * unit,
        scalars=2,
        scratch=[pltpu.VMEM((2, 4 * n, 2 * n), f32)],
    )
    passed = send(narrow(across), ACROSS)
    swapped = send(narrow(sum_1), OTHER_CORE)
    sum_a, sum_b, sum_2 = call(
        text_body,
        [((n, width), f32)] * 2 + [((2 * n, width), f32)],
        (images, w0, weights),
        4 * unit,
        scalars=0,
    )
    passed = wide(passed)
    swapped = wide(swapped)
    to_first = jnp.where(first_core, swapped, 0.0)
    sum_b = sum_b + to_first[n:]
    sum_2 = sum_2 + jnp.where(first_core, 0.0, swapped)
    loss_o = send(loss, OTHER_CORE)
    out = lax.optimization_barrier(
        tuple(narrow(v) for v in (sum_b, sum_2[:n], sum_2[n:])) + (sum_a + to_first[:n], w0)
    )
    sum_a, w0 = out[3:]
    out = out[:3]
    own, left, right = call(
        image_body, [((n, width), f32)] * 3, (w0, weights, t0, text), 9 * unit // 2, scalars=0
    )
    left = left + jnp.where(first_core, 0.0, passed)
    right = right + jnp.where(first_core, passed, 0.0)
    out = out + lax.optimization_barrier((narrow(left), narrow(right), loss, loss_o))
    (loss,) = call(spread_body, [((CHIP_COUNT, 1, 128), f32)], out[5:], 4, scalars=0)
    out = out[:5] + (loss,)
    back_z = send(out[0], along_z(2))
    back_a = send(out[1], next_column(-1, lambda core: 0))
    back_b = send(out[2], next_column(-1, lambda core: 1))
    home_l = send(out[3], along_x(-1))
    home_r = send(out[4], along_x(1))

    losses = lax.all_to_all(out[5], CHIPS, 0, 0, tiled=True)
    text_out = scale * (sum_a + wide(back_z) + wide(back_a) + wide(back_b))
    own, text_out = lax.optimization_barrier((own, text_out))
    image_out = scale * (own + wide(home_l) + wide(home_r))
    losses, image_out = lax.optimization_barrier((losses, image_out))
    pair_count = DEVICES * n * 3 * 8 * n
    mean_loss = pl.pallas_call(
        functools.partial(mean_body, pair_count),
        out_shape=jax.ShapeDtypeStruct((1,), f32),
        in_specs=[WHOLE],
        out_specs=SCALAR,
    )(losses)
    return image_out, text_out, mean_loss


def solution(mesh):
    fine = Mesh(mesh.devices.reshape(NY, 2, 2, NX, 2), AXES)
    placed = (P(AXES, None), P(AXES, None), P(), P())
    return jax.shard_map(
        local,
        mesh=fine,
        in_specs=placed,
        out_specs=(P(AXES, None), P(AXES, None), P()),
        check_vma=False,
    )
```

```python
import functools

import jax
import jax.numpy as jnp
from jax import lax
from jax.experimental import pallas as pl
from jax.experimental.pallas import tpu as pltpu
from jax.sharding import Mesh
from jax.sharding import PartitionSpec as P

AXES = ("y", "z_lo", "core", "x", "z_hi")
CHIPS = ("y", "z_lo", "x", "z_hi")
NY, NX = 4, 4
DEVICES = 128
CHIP_COUNT = 64
SEND_SCALE = 64.0
TILE = 64
LAST = (((1,), (1,)), ((), ()))
FIRST = (((0,), (0,)), ((), ()))
PLAIN = (((1,), (0,)), ((), ()))
VMEM_BYTES = 16 * 1024 * 1024


def place(y, z, core, x):
    z = z % 4
    return (((y % NY) * 2 + z % 2) * 2 + core % 2) * 8 + (x % NX) * 2 + z // 2


def route(move):
    pairs = []
    for y in range(NY):
        for z in range(4):
            for core in range(2):
                for x in range(NX):
                    pairs.append((place(y, z, core, x), place(*move(y, z, core, x))))
    return pairs


def along_x(k):
    return route(lambda y, z, core, x: (y, z, core, x + k))


def along_z(k):
    return route(lambda y, z, core, x: (y, z + k, core, x))


def next_column(k, flip_zh):
    def move(y, z, core, x):
        zh, zl = z // 2, z % 2
        column = (y * 2 + zl + k) % 8
        return column // 2, (zh ^ flip_zh(core)) * 2 + column % 2, core, x

    return route(move)


AHEAD = route(lambda y, z, core, x: (y, z, core, x + 1 - 2 * core))
BEHIND = route(lambda y, z, core, x: (y, z, core, x - 1 + 2 * core))
OTHER_CORE = route(lambda y, z, core, x: (y, z, core + 1, x))


def send(value, pairs):
    return lax.ppermute(value, AXES, pairs)


def dot(a, b, dims):
    return lax.dot_general(a, b, dims, preferred_element_type=jnp.float32)


WHOLE = pl.BlockSpec(memory_space=pltpu.VMEM)
SCALAR = pl.BlockSpec(memory_space=pltpu.SMEM)


def call(body, outs, ins, flops, scalars=1, scratch=()):
    return pl.pallas_call(
        body,
        out_shape=tuple(jax.ShapeDtypeStruct(s, t) for s, t in outs),
        in_specs=[SCALAR] * scalars + [WHOLE] * (len(ins) - scalars),
        out_specs=(WHOLE,) * len(outs),
        scratch_shapes=scratch,
        compiler_params=pltpu.CompilerParams(vmem_limit_bytes=VMEM_BYTES),
        cost_estimate=pl.CostEstimate(
            flops=flops, bytes_accessed=1 << 20, transcendentals=0
        ),
    )(*ins)


def tile_terms(scalars, z, match):
    z = scalars[0] * z + scalars[1]
    e = jnp.exp(-jnp.abs(z))
    d = 1.0 + e
    r = pltpu.reciprocal(d, approx=True)
    r = r * (2.0 - d * r)
    p = r * jnp.where(z >= 0.0, 1.0, e)
    top = jnp.maximum(z, 0.0)
    if match is not None:
        p = p - match
        top = top - match * z
    rows, cols = z.shape
    total = jnp.sum(top.reshape(rows // 8, 8, cols), axis=0)
    e = e.reshape(rows // 8, 8, cols)
    d = d.reshape(rows // 8, 8, cols)
    q = e[0]
    for k in range(1, rows // 8):
        q = q * d[k] + e[k]
    return p.astype(jnp.bfloat16), total + jnp.log1p(q)


def pair_weights(scalars, images, text, weights, products, loss, labelled):
    step = products.shape[2]
    rows, cols = weights.shape
    own = rows // 2

    def multiply(k):
        products[k % 2, :, :] = dot(text, images[pl.ds(k * step, step), :], LAST)

    multiply(0)
    for k in range(cols // step):
        if (k + 1) * step < cols:
            multiply(k + 1)
        for r in range(0, rows, TILE):
            for c in range(0, step, 128):
                match = None
                at = k * step + c
                if labelled and r < own and at < own and at < r + TILE and r < at + 128:
                    row = lax.broadcasted_iota(jnp.int32, (TILE, 128), 0) + r
                    col = lax.broadcasted_iota(jnp.int32, (TILE, 128), 1) + at
                    match = ((row == col) & (row < own)).astype(jnp.float32)
                part, terms = tile_terms(
                    scalars, products[k % 2, pl.ds(r, TILE), pl.ds(c, 128)], match
                )
                weights[pl.ds(r, TILE), pl.ds(at, 128)] = part
                loss = loss + terms
    return loss


def near_body(scalars, i0, i1, i2, i3, ta, tb, images, text, weights, loss, products):
    n = ta.shape[0]
    for k, ref in enumerate((i0, i1, i2, i3)):
        images[pl.ds(k * n, n), :] = ref[...]
    text[pl.ds(0, n), :] = ta[...]
    text[pl.ds(n, n), :] = tb[...]
    none = jnp.zeros((8, 128), jnp.float32)
    loss[...] = pair_weights(scalars, images, text[...], weights, products, none, True)


def far_body(scalars, core, images, t0, w0, own_o, z_o, far, far_o, loss_0, text, weights, across, sum_1, loss, products):
    n = own_o.shape[0]
    low, high, last = pl.ds(0, n), pl.ds(n, n), pl.ds(3 * n, n)
    first = core[0] == 0
    text[pl.ds(0, n), :] = jnp.where(first, far[high, :], own_o[...])
    text[pl.ds(n, n), :] = jnp.where(first, far_o[high, :], z_o[...])
    text[pl.ds(2 * n, n), :] = jnp.where(first, far[low, :], far_o[high, :])
    text[pl.ds(3 * n, n), :] = jnp.where(first, far_o[low, :], far[high, :])
    loss[...] = pair_weights(scalars, images, text[...], weights, products, loss_0[...], False)
    sum_1[...] = dot(weights[pl.ds(0, 2 * n), :], images[...], PLAIN)
    across[...] = dot(w0[:, last], t0[...], FIRST) + dot(weights[:, last], text[...], FIRST)


def text_body(images, w0, weights, sum_a, sum_b, sum_2):
    n = sum_a.shape[0]
    out = dot(w0[...], images[...], PLAIN)
    sum_a[...] = out[:n]
    sum_b[...] = out[n:]
    sum_2[...] = dot(weights[pl.ds(2 * n, 2 * n), :], images[...], PLAIN)


def image_body(w0, weights, t0, text, *outs):
    n = outs[0].shape[0]
    cut = pl.ds(0, len(outs) * n)
    out = dot(w0[:, cut], t0[...], FIRST) + dot(weights[:, cut], text[...], FIRST)
    for k, ref in enumerate(outs):
        ref[...] = out[k * n : (k + 1) * n]


def spread_body(mine, other, out):
    total = jnp.sum(mine[...] + other[...])
    out[...] = jnp.full(out.shape, total, jnp.float32)


def mean_body(pairs, parts, out):
    out[0] = jnp.sum(parts[...][:, 0, :1]) / pairs


def narrow(value):
    return (value * SEND_SCALE).astype(jnp.float16)


def wide(value):
    return value.astype(jnp.float32) * (1.0 / SEND_SCALE)


def local(image_embed, text_embed, scale_parameter, logit_bias):
    n, width = image_embed.shape
    scale = scale_parameter[0]
    scalars = jnp.concatenate([scale_parameter, logit_bias])
    core = lax.axis_index("core").astype(jnp.int32).reshape(1)
    first_core = core[0] == 0
    bf16, f32 = jnp.bfloat16, jnp.float32
    unit = 2 * n * 4 * n * width

    text_b = text_embed.astype(bf16)
    image_b = image_embed.astype(bf16)
    text_o = send(text_b, OTHER_CORE)
    both = jnp.where(
        first_core,
        jnp.concatenate([text_b, text_o]),
        jnp.concatenate([text_o, text_b]),
    )
    far = send(both, next_column(1, lambda core: core))
    text_z = send(text_b, along_z(2))
    image_l = send(image_b, AHEAD)
    image_r = send(image_b, BEHIND)
    image_f = send(image_b, along_x(2))
    far, text_z, image_l, image_r, image_f, scalars, core = lax.optimization_barrier(
        (far, text_z, image_l, image_r, image_f, scalars, core)
    )
    z_o = send(text_z, OTHER_CORE)
    far_o = send(far, OTHER_CORE)

    images, t0, w0, loss_0 = call(
        near_body,
        [((4 * n, width), bf16), ((2 * n, width), bf16), ((2 * n, 4 * n), bf16), ((8, 128), f32)],
        (scalars, image_b, image_l, image_r, image_f, text_b, text_z),
        2 * unit,
        scratch=[pltpu.VMEM((2, 2 * n, 2 * n), f32)],
    )
    text, weights, across, sum_1, loss = call(
        far_body,
        [
            ((4 * n, width), bf16),
            ((4 * n, 4 * n), bf16),
            ((n, width), f32),
            ((2 * n, width), f32),
            ((8, 128), f32),
        ],
        (scalars, core, images, t0, w0, text_o, z_o, far, far_o, loss_0),
        8 * unit,
        scalars=2,
        scratch=[pltpu.VMEM((2, 4 * n, 2 * n), f32)],
    )
    passed = send(narrow(across), AHEAD)
    swapped = send(narrow(sum_1), OTHER_CORE)
    sum_a, sum_b, sum_2 = call(
        text_body,
        [((n, width), f32)] * 2 + [((2 * n, width), f32)],
        (images, w0, weights),
        4 * unit,
        scalars=0,
    )
    passed = wide(passed)
    swapped = wide(swapped)
    to_first = jnp.where(first_core, swapped, 0.0)
    sum_b = sum_b + to_first[n:]
    sum_2 = sum_2 + jnp.where(first_core, 0.0, swapped)
    loss_o = send(loss, OTHER_CORE)
    out = lax.optimization_barrier(
        tuple(narrow(v) for v in (sum_b, sum_2[:n], sum_2[n:])) + (sum_a + to_first[:n], w0)
    )
    sum_a, w0 = out[3:]
    out = out[:3]
    own, left, right = call(
        image_body, [((n, width), f32)] * 3, (w0, weights, t0, text), 9 * unit // 2, scalars=0
    )
    right = right + passed
    out = out + lax.optimization_barrier((narrow(left), narrow(right), loss, loss_o))
    (loss,) = call(spread_body, [((CHIP_COUNT, 1, 128), f32)], out[5:], 4, scalars=0)
    out = out[:5] + (loss,)
    back_z = send(out[0], along_z(2))
    back_a = send(out[1], next_column(-1, lambda core: 0))
    back_b = send(out[2], next_column(-1, lambda core: 1))
    home_l = send(out[3], BEHIND)
    home_r = send(out[4], AHEAD)

    losses = lax.all_to_all(out[5], CHIPS, 0, 0, tiled=True)
    text_out = scale * (sum_a + wide(back_z) + wide(back_a) + wide(back_b))
    own, text_out = lax.optimization_barrier((own, text_out))
    image_out = scale * (own + wide(home_l) + wide(home_r))
    losses, image_out = lax.optimization_barrier((losses, image_out))
    pair_count = DEVICES * n * 3 * 8 * n
    mean_loss = pl.pallas_call(
        functools.partial(mean_body, pair_count),
        out_shape=jax.ShapeDtypeStruct((1,), f32),
        in_specs=[WHOLE],
        out_specs=SCALAR,
    )(losses)
    return image_out, text_out, mean_loss


def solution(mesh):
    fine = Mesh(mesh.devices.reshape(NY, 2, 2, NX, 2), AXES)
    placed = (P(AXES, None), P(AXES, None), P(), P())
    return jax.shard_map(
        local,
        mesh=fine,
        in_specs=placed,
        out_specs=(P(AXES, None), P(AXES, None), P()),
        check_vma=False,
    )
```

```python
import functools

import jax
import jax.numpy as jnp
from jax import lax
from jax.experimental import pallas as pl
from jax.experimental.pallas import tpu as pltpu
from jax.sharding import Mesh
from jax.sharding import PartitionSpec as P

AXES = ("y", "z_lo", "core", "x", "z_hi")
CHIPS = ("y", "z_lo", "x", "z_hi")
NY, NX = 4, 4
DEVICES = 128
CHIP_COUNT = 64
SEND_SCALE = 64.0
TILE = 64
LAST = (((1,), (1,)), ((), ()))
FIRST = (((0,), (0,)), ((), ()))
PLAIN = (((1,), (0,)), ((), ()))
VMEM_BYTES = 12 * 1024 * 1024


def place(y, z, core, x):
    z = z % 4
    return (((y % NY) * 2 + z % 2) * 2 + core % 2) * 8 + (x % NX) * 2 + z // 2


def route(move):
    pairs = []
    for y in range(NY):
        for z in range(4):
            for core in range(2):
                for x in range(NX):
                    pairs.append((place(y, z, core, x), place(*move(y, z, core, x))))
    return pairs


def along_x(k):
    return route(lambda y, z, core, x: (y, z, core, x + k))


def along_z(k):
    return route(lambda y, z, core, x: (y, z + k, core, x))


def next_column(k, flip_zh):
    def move(y, z, core, x):
        zh, zl = z // 2, z % 2
        column = (y * 2 + zl + k) % 8
        return column // 2, (zh ^ flip_zh(core)) * 2 + column % 2, core, x

    return route(move)


AHEAD = route(lambda y, z, core, x: (y, z, core, x + 1 - 2 * core))
BEHIND = route(lambda y, z, core, x: (y, z, core, x - 1 + 2 * core))
OTHER_CORE = route(lambda y, z, core, x: (y, z, core + 1, x))


def send(value, pairs):
    return lax.ppermute(value, AXES, pairs)


def dot(a, b, dims):
    return lax.dot_general(a, b, dims, preferred_element_type=jnp.float32)


WHOLE = pl.BlockSpec(memory_space=pltpu.VMEM)
SCALAR = pl.BlockSpec(memory_space=pltpu.SMEM)


def call(body, outs, ins, flops, scalars=1, scratch=()):
    return pl.pallas_call(
        body,
        out_shape=tuple(jax.ShapeDtypeStruct(s, t) for s, t in outs),
        in_specs=[SCALAR] * scalars + [WHOLE] * (len(ins) - scalars),
        out_specs=(WHOLE,) * len(outs),
        scratch_shapes=scratch,
        compiler_params=pltpu.CompilerParams(vmem_limit_bytes=VMEM_BYTES),
        cost_estimate=pl.CostEstimate(
            flops=flops, bytes_accessed=1 << 20, transcendentals=0
        ),
    )(*ins)


def tile_terms(scalars, z, match):
    z = scalars[0] * z + scalars[1]
    e = jnp.exp(-jnp.abs(z))
    d = 1.0 + e
    r = pltpu.reciprocal(d, approx=True)
    r = r * (2.0 - d * r)
    p = r * jnp.where(z >= 0.0, 1.0, e)
    top = jnp.maximum(z, 0.0)
    if match is not None:
        p = p - match
        top = top - match * z
    rows, cols = z.shape
    total = jnp.sum(top.reshape(rows // 8, 8, cols), axis=0)
    e = e.reshape(rows // 8, 8, cols)
    d = d.reshape(rows // 8, 8, cols)
    q = e[0]
    for k in range(1, rows // 8):
        q = q * d[k] + e[k]
    return p.astype(jnp.bfloat16), total + jnp.log1p(q)


def pair_weights(scalars, images, text, weights, products, loss, labelled):
    step = products.shape[2]
    rows, cols = weights.shape
    own = rows // 2

    def multiply(k):
        products[k % 2, :, :] = dot(text, images[pl.ds(k * step, step), :], LAST)

    multiply(0)
    for k in range(cols // step):
        if (k + 1) * step < cols:
            multiply(k + 1)
        for r in range(0, rows, TILE):
            for c in range(0, step, 128):
                match = None
                at = k * step + c
                if labelled and r < own and at < own and at < r + TILE and r < at + 128:
                    row = lax.broadcasted_iota(jnp.int32, (TILE, 128), 0) + r
                    col = lax.broadcasted_iota(jnp.int32, (TILE, 128), 1) + at
                    match = ((row == col) & (row < own)).astype(jnp.float32)
                part, terms = tile_terms(
                    scalars, products[k % 2, pl.ds(r, TILE), pl.ds(c, 128)], match
                )
                weights[pl.ds(r, TILE), pl.ds(at, 128)] = part
                loss = loss + terms
    return loss


def near_body(scalars, i0, i1, i2, i3, ta, tb, images, text, weights, loss, products):
    n = ta.shape[0]
    for k, ref in enumerate((i0, i1, i2, i3)):
        images[pl.ds(k * n, n), :] = ref[...]
    text[pl.ds(0, n), :] = ta[...]
    text[pl.ds(n, n), :] = tb[...]
    none = jnp.zeros((8, 128), jnp.float32)
    loss[...] = pair_weights(scalars, images, text[...], weights, products, none, True)


def far_body(scalars, core, images, t0, w0, own_o, z_o, far, far_o, loss_0, text, weights, across, sum_1, loss, products):
    n = own_o.shape[0]
    low, high, last = pl.ds(0, n), pl.ds(n, n), pl.ds(3 * n, n)
    first = core[0] == 0
    text[pl.ds(0, n), :] = jnp.where(first, far[high, :], own_o[...])
    text[pl.ds(n, n), :] = jnp.where(first, far_o[high, :], z_o[...])
    text[pl.ds(2 * n, n), :] = jnp.where(first, far[low, :], far_o[high, :])
    text[pl.ds(3 * n, n), :] = jnp.where(first, far_o[low, :], far[high, :])
    loss[...] = pair_weights(scalars, images, text[...], weights, products, loss_0[...], False)
    sum_1[...] = dot(weights[pl.ds(0, 2 * n), :], images[...], PLAIN)
    across[...] = dot(w0[:, last], t0[...], FIRST) + dot(weights[:, last], text[...], FIRST)


def text_body(images, w0, weights, sum_a, sum_b, sum_2):
    n = sum_a.shape[0]
    out = dot(w0[...], images[...], PLAIN)
    sum_a[...] = out[:n]
    sum_b[...] = out[n:]
    sum_2[...] = dot(weights[pl.ds(2 * n, 2 * n), :], images[...], PLAIN)


def image_body(w0, weights, t0, text, loss, loss_o, spread, *outs):
    spread[...] = jnp.full(spread.shape, jnp.sum(loss[...] + loss_o[...]), jnp.float32)
    n = outs[0].shape[0]
    cut = pl.ds(0, len(outs) * n)
    out = dot(w0[:, cut], t0[...], FIRST) + dot(weights[:, cut], text[...], FIRST)
    for k, ref in enumerate(outs):
        ref[...] = out[k * n : (k + 1) * n]


def mean_body(pairs, parts, out):
    out[0] = jnp.sum(parts[...][:, 0, :1]) / pairs


def narrow(value):
    return (value * SEND_SCALE).astype(jnp.float16)


def wide(value):
    return value.astype(jnp.float32) * (1.0 / SEND_SCALE)


def local(image_embed, text_embed, scale_parameter, logit_bias):
    n, width = image_embed.shape
    scale = scale_parameter[0]
    scalars = jnp.concatenate([scale_parameter, logit_bias])
    core = lax.axis_index("core").astype(jnp.int32).reshape(1)
    first_core = core[0] == 0
    bf16, f32 = jnp.bfloat16, jnp.float32
    unit = 2 * n * 4 * n * width

    text_b = text_embed.astype(bf16)
    image_b = image_embed.astype(bf16)
    text_o = send(text_b, OTHER_CORE)
    both = jnp.where(
        first_core,
        jnp.concatenate([text_b, text_o]),
        jnp.concatenate([text_o, text_b]),
    )
    far = send(both, next_column(1, lambda core: core))
    text_z = send(text_b, along_z(2))
    image_l = send(image_b, AHEAD)
    image_r = send(image_b, BEHIND)
    image_f = send(image_b, along_x(2))
    far, text_z, image_l, image_r, image_f, scalars, core = lax.optimization_barrier(
        (far, text_z, image_l, image_r, image_f, scalars, core)
    )
    z_o = send(text_z, OTHER_CORE)
    far_o = send(far, OTHER_CORE)

    images, t0, w0, loss_0 = call(
        near_body,
        [((4 * n, width), bf16), ((2 * n, width), bf16), ((2 * n, 4 * n), bf16), ((8, 128), f32)],
        (scalars, image_b, image_l, image_r, image_f, text_b, text_z),
        2 * unit,
        scratch=[pltpu.VMEM((2, 2 * n, 2 * n), f32)],
    )
    text, weights, across, sum_1, loss = call(
        far_body,
        [
            ((4 * n, width), bf16),
            ((4 * n, 4 * n), bf16),
            ((n, width), f32),
            ((2 * n, width), f32),
            ((8, 128), f32),
        ],
        (scalars, core, images, t0, w0, text_o, z_o, far, far_o, loss_0),
        8 * unit,
        scalars=2,
        scratch=[pltpu.VMEM((2, 4 * n, 2 * n), f32)],
    )
    passed = send(narrow(across), AHEAD)
    swapped = send(narrow(sum_1), OTHER_CORE)
    sum_a, sum_b, sum_2 = call(
        text_body,
        [((n, width), f32)] * 2 + [((2 * n, width), f32)],
        (images, w0, weights),
        4 * unit,
        scalars=0,
    )
    passed = wide(passed)
    swapped = wide(swapped)
    to_first = jnp.where(first_core, swapped, 0.0)
    sum_b = sum_b + to_first[n:]
    sum_2 = sum_2 + jnp.where(first_core, 0.0, swapped)
    loss_o = send(loss, OTHER_CORE)
    out = lax.optimization_barrier(
        tuple(narrow(v) for v in (sum_b, sum_2[:n], sum_2[n:])) + (sum_a + to_first[:n], w0)
    )
    sum_a, w0 = out[3:]
    out = out[:3]
    loss, own, left, right = call(
        image_body,
        [((CHIP_COUNT, 1, 128), f32)] + [((n, width), f32)] * 3,
        (w0, weights, t0, text, loss, loss_o),
        9 * unit // 2,
        scalars=0,
    )
    right = right + passed
    out = out + lax.optimization_barrier((narrow(left), narrow(right), loss))
    back_z = send(out[0], along_z(2))
    back_a = send(out[1], next_column(-1, lambda core: 0))
    back_b = send(out[2], next_column(-1, lambda core: 1))
    home_l = send(out[3], BEHIND)
    home_r = send(out[4], AHEAD)

    losses = lax.all_to_all(out[5], CHIPS, 0, 0, tiled=True)
    text_out = scale * (sum_a + wide(back_z) + wide(back_a) + wide(back_b))
    own, text_out = lax.optimization_barrier((own, text_out))
    image_out = scale * (own + wide(home_l) + wide(home_r))
    losses, image_out = lax.optimization_barrier((losses, image_out))
    pair_count = DEVICES * n * 3 * 8 * n
    mean_loss = pl.pallas_call(
        functools.partial(mean_body, pair_count),
        out_shape=jax.ShapeDtypeStruct((1,), f32),
        in_specs=[WHOLE],
        out_specs=SCALAR,
    )(losses)
    return image_out, text_out, mean_loss


def solution(mesh):
    fine = Mesh(mesh.devices.reshape(NY, 2, 2, NX, 2), AXES)
    placed = (P(AXES, None), P(AXES, None), P(), P())
    return jax.shard_map(
        local,
        mesh=fine,
        in_specs=placed,
        out_specs=(P(AXES, None), P(AXES, None), P()),
        check_vma=False,
    )
```

```python
import functools

import jax
import jax.numpy as jnp
from jax import lax
from jax.experimental import pallas as pl
from jax.experimental.pallas import tpu as pltpu
from jax.sharding import Mesh
from jax.sharding import PartitionSpec as P

AXES = ("y", "z_lo", "core", "x", "z_hi")
CHIPS = ("y", "z_lo", "x", "z_hi")
NY, NX = 4, 4
DEVICES = 128
CHIP_COUNT = 64
SEND_SCALE = 64.0
TILE = 64
LAST = (((1,), (1,)), ((), ()))
FIRST = (((0,), (0,)), ((), ()))
PLAIN = (((1,), (0,)), ((), ()))
VMEM_BYTES = 12 * 1024 * 1024


def place(y, z, core, x):
    z = z % 4
    return (((y % NY) * 2 + z % 2) * 2 + core % 2) * 8 + (x % NX) * 2 + z // 2


def route(move):
    pairs = []
    for y in range(NY):
        for z in range(4):
            for core in range(2):
                for x in range(NX):
                    pairs.append((place(y, z, core, x), place(*move(y, z, core, x))))
    return pairs


def along_x(k):
    return route(lambda y, z, core, x: (y, z, core, x + k))


def along_z(k):
    return route(lambda y, z, core, x: (y, z + k, core, x))


def next_column(k, flip_zh):
    def move(y, z, core, x):
        zh, zl = z // 2, z % 2
        column = (y * 2 + zl + k) % 8
        return column // 2, (zh ^ flip_zh(core)) * 2 + column % 2, core, x

    return route(move)


AHEAD = route(lambda y, z, core, x: (y, z, core, x + 1 - 2 * core))
BEHIND = route(lambda y, z, core, x: (y, z, core, x - 1 + 2 * core))
OTHER_CORE = route(lambda y, z, core, x: (y, z, core + 1, x))


def send(value, pairs):
    return lax.ppermute(value, AXES, pairs)


def dot(a, b, dims):
    return lax.dot_general(a, b, dims, preferred_element_type=jnp.float32)


WHOLE = pl.BlockSpec(memory_space=pltpu.VMEM)
SCALAR = pl.BlockSpec(memory_space=pltpu.SMEM)


def call(body, outs, ins, flops, scalars=1, scratch=()):
    return pl.pallas_call(
        body,
        out_shape=tuple(jax.ShapeDtypeStruct(s, t) for s, t in outs),
        in_specs=[SCALAR] * scalars + [WHOLE] * (len(ins) - scalars),
        out_specs=(WHOLE,) * len(outs),
        scratch_shapes=scratch,
        compiler_params=pltpu.CompilerParams(vmem_limit_bytes=VMEM_BYTES),
        cost_estimate=pl.CostEstimate(
            flops=flops, bytes_accessed=1 << 20, transcendentals=0
        ),
    )(*ins)


def tile_terms(scalars, z, match):
    z = scalars[0] * z + scalars[1]
    e = jnp.exp(-jnp.abs(z))
    d = 1.0 + e
    r = pltpu.reciprocal(d, approx=True)
    r = r * (2.0 - d * r)
    p = r * jnp.where(z >= 0.0, 1.0, e)
    top = jnp.maximum(z, 0.0)
    if match is not None:
        p = p - match
        top = top - match * z
    rows, cols = z.shape
    total = jnp.sum(top.reshape(rows // 8, 8, cols), axis=0)
    e = e.reshape(rows // 8, 8, cols)
    d = d.reshape(rows // 8, 8, cols)
    q = e[0]
    for k in range(1, rows // 8):
        q = q * d[k] + e[k]
    return p.astype(jnp.bfloat16), total + jnp.log1p(q)


def pair_weights(scalars, images, text, weights, products, loss, labelled):
    step = products.shape[2]
    rows, cols = weights.shape
    own = rows // 2

    def multiply(k):
        products[k % 2, :, :] = dot(text, images[pl.ds(k * step, step), :], LAST)

    multiply(0)
    for k in range(cols // step):
        if (k + 1) * step < cols:
            multiply(k + 1)
        for r in range(0, rows, TILE):
            for c in range(0, step, 128):
                match = None
                at = k * step + c
                if labelled and r < own and at < own and at < r + TILE and r < at + 128:
                    row = lax.broadcasted_iota(jnp.int32, (TILE, 128), 0) + r
                    col = lax.broadcasted_iota(jnp.int32, (TILE, 128), 1) + at
                    match = ((row == col) & (row < own)).astype(jnp.float32)
                part, terms = tile_terms(
                    scalars, products[k % 2, pl.ds(r, TILE), pl.ds(c, 128)], match
                )
                weights[pl.ds(r, TILE), pl.ds(at, 128)] = part
                loss = loss + terms
    return loss


def near_body(scalars, i0, i1, i2, i3, ta, tb, images, text, weights, loss, products):
    n = ta.shape[0]
    for k, ref in enumerate((i0, i1, i2, i3)):
        images[pl.ds(k * n, n), :] = ref[...]
    text[pl.ds(0, n), :] = ta[...]
    text[pl.ds(n, n), :] = tb[...]
    none = jnp.zeros((8, 128), jnp.float32)
    loss[...] = pair_weights(scalars, images, text[...], weights, products, none, True)


def far_body(scalars, core, images, t0, w0, own_o, z_o, far, far_o, loss_0, text, weights, across, sum_1, loss, products):
    n = own_o.shape[0]
    low, high, last = pl.ds(0, n), pl.ds(n, n), pl.ds(3 * n, n)
    first = core[0] == 0
    text[pl.ds(0, n), :] = jnp.where(first, far[high, :], own_o[...])
    text[pl.ds(n, n), :] = jnp.where(first, far_o[high, :], z_o[...])
    text[pl.ds(2 * n, n), :] = jnp.where(first, far[low, :], far_o[high, :])
    text[pl.ds(3 * n, n), :] = jnp.where(first, far_o[low, :], far[high, :])
    loss[...] = pair_weights(scalars, images, text[...], weights, products, loss_0[...], False)
    sum_1[...] = dot(weights[pl.ds(0, 2 * n), :], images[...], PLAIN)
    across[...] = dot(w0[:, last], t0[...], FIRST) + dot(weights[:, last], text[...], FIRST)


def text_body(images, w0, weights, sum_a, sum_b, sum_2):
    n = sum_a.shape[0]
    out = dot(w0[...], images[...], PLAIN)
    sum_a[...] = out[:n]
    sum_b[...] = out[n:]
    sum_2[...] = dot(weights[pl.ds(2 * n, 2 * n), :], images[...], PLAIN)


def image_body(w0, weights, t0, text, loss, loss_o, spread, *outs):
    spread[...] = jnp.full(spread.shape, jnp.sum(loss[...] + loss_o[...]), jnp.float32)
    n = outs[0].shape[0]
    cut = pl.ds(0, len(outs) * n)
    out = dot(w0[:, cut], t0[...], FIRST) + dot(weights[:, cut], text[...], FIRST)
    for k, ref in enumerate(outs):
        ref[...] = out[k * n : (k + 1) * n]


def mean_body(pairs, parts, out):
    out[0] = jnp.sum(parts[...][:, 0, :1]) / pairs


def narrow(value):
    return (value * SEND_SCALE).astype(jnp.float16)


def wide(value):
    return value.astype(jnp.float32) * (1.0 / SEND_SCALE)


def local(image_embed, text_embed, scale_parameter, logit_bias):
    n, width = image_embed.shape
    scale = scale_parameter[0]
    scalars = jnp.concatenate([scale_parameter, logit_bias])
    core = lax.axis_index("core").astype(jnp.int32).reshape(1)
    first_core = core[0] == 0
    bf16, f32 = jnp.bfloat16, jnp.float32
    unit = 2 * n * 4 * n * width

    text_b = text_embed.astype(bf16)
    image_b = image_embed.astype(bf16)
    text_o = send(text_b, OTHER_CORE)
    both = jnp.where(
        first_core,
        jnp.concatenate([text_b, text_o]),
        jnp.concatenate([text_o, text_b]),
    )
    far = send(both, next_column(1, lambda core: core))
    text_z = send(text_b, along_z(2))
    image_l = send(image_b, AHEAD)
    image_r = send(image_b, BEHIND)
    image_f = send(image_b, along_x(2))
    far, text_z, image_l, image_r, image_f, scalars, core = lax.optimization_barrier(
        (far, text_z, image_l, image_r, image_f, scalars, core)
    )
    z_o = send(text_z, OTHER_CORE)
    far_o = send(far, OTHER_CORE)

    images, t0, w0, loss_0 = call(
        near_body,
        [((4 * n, width), bf16), ((2 * n, width), bf16), ((2 * n, 4 * n), bf16), ((8, 128), f32)],
        (scalars, image_b, image_l, image_r, image_f, text_b, text_z),
        2 * unit,
        scratch=[pltpu.VMEM((1, 2 * n, 4 * n), f32)],
    )
    text, weights, across, sum_1, loss = call(
        far_body,
        [
            ((4 * n, width), bf16),
            ((4 * n, 4 * n), bf16),
            ((n, width), f32),
            ((2 * n, width), f32),
            ((8, 128), f32),
        ],
        (scalars, core, images, t0, w0, text_o, z_o, far, far_o, loss_0),
        8 * unit,
        scalars=2,
        scratch=[pltpu.VMEM((2, 4 * n, 2 * n), f32)],
    )
    passed = send(narrow(across), AHEAD)
    swapped = send(narrow(sum_1), OTHER_CORE)
    sum_a, sum_b, sum_2 = call(
        text_body,
        [((n, width), f32)] * 2 + [((2 * n, width), f32)],
        (images, w0, weights),
        4 * unit,
        scalars=0,
    )
    passed = wide(passed)
    swapped = wide(swapped)
    to_first = jnp.where(first_core, swapped, 0.0)
    sum_b = sum_b + to_first[n:]
    sum_2 = sum_2 + jnp.where(first_core, 0.0, swapped)
    loss_o = send(loss, OTHER_CORE)
    out = lax.optimization_barrier(
        tuple(narrow(v) for v in (sum_b, sum_2[:n], sum_2[n:])) + (sum_a + to_first[:n], w0)
    )
    sum_a, w0 = out[3:]
    out = out[:3]
    loss, own, left, right = call(
        image_body,
        [((CHIP_COUNT, 1, 128), f32)] + [((n, width), f32)] * 3,
        (w0, weights, t0, text, loss, loss_o),
        9 * unit // 2,
        scalars=0,
    )
    right = right + passed
    out = out + lax.optimization_barrier((narrow(left), narrow(right), loss))
    back_z = send(out[0], along_z(2))
    back_a = send(out[1], next_column(-1, lambda core: 0))
    back_b = send(out[2], next_column(-1, lambda core: 1))
    home_l = send(out[3], BEHIND)
    home_r = send(out[4], AHEAD)

    losses = lax.all_to_all(out[5], CHIPS, 0, 0, tiled=True)
    text_out = scale * (sum_a + wide(back_z) + wide(back_a) + wide(back_b))
    own, text_out = lax.optimization_barrier((own, text_out))
    image_out = scale * (own + wide(home_l) + wide(home_r))
    losses, image_out = lax.optimization_barrier((losses, image_out))
    pair_count = DEVICES * n * 3 * 8 * n
    mean_loss = pl.pallas_call(
        functools.partial(mean_body, pair_count),
        out_shape=jax.ShapeDtypeStruct((1,), f32),
        in_specs=[WHOLE],
        out_specs=SCALAR,
    )(losses)
    return image_out, text_out, mean_loss


def solution(mesh):
    fine = Mesh(mesh.devices.reshape(NY, 2, 2, NX, 2), AXES)
    placed = (P(AXES, None), P(AXES, None), P(), P())
    return jax.shard_map(
        local,
        mesh=fine,
        in_specs=placed,
        out_specs=(P(AXES, None), P(AXES, None), P()),
        check_vma=False,
    )
```
